32 devices in a mesh: grp: 2 (over x), row: 16 (over z, y, core).
Axes of the slice: x: 2, y: 2, z: 4, core: 2. Of those that a mesh axis runs over, the one named last changes fastest.
Arguments:
- images: bfloat16 [512, 512, 128], P(('grp', 'row')), parts along dimension 0, may hold values from -6 to 6
- weight_one: bfloat16 [3, 3, 128, 256], replicated, may hold values from -0.1875 to 0.1875
- bias_one: float32 [256], replicated, may hold values from -3 to 3
- weight_two: bfloat16 [3, 3, 256, 256], replicated, may hold values from -0.125 to 0.125
- bias_two: float32 [256], replicated, may hold values from -3 to 3
- cotangent: bfloat16 [256, 256, 256], P(('grp', 'row')), parts along dimension 0, may hold values from -0.0234375 to 0.0234375
Outputs:
- coarse_out: bfloat16 [256, 256, 256], P(('grp', 'row')), parts along dimension 0
- grad_w_one: float32 [6, 3, 128, 256], P('grp'), parts along dimension 0
- grad_b_one: float32 [512], P('grp'), parts along dimension 0
- grad_w_two: float32 [6, 3, 256, 256], P('grp'), parts along dimension 0
- grad_b_two: float32 [512], P('grp'), parts along dimension 0
The draws below stay inside these ranges and needn't reach their ends.
There are 2 independent parts, one for each index of `grp`. The reference program is written for one: setup_inputs(seed, part) draws one part's arguments, and reference() takes and returns one part's arrays. A program takes and returns all parts, laid end to end along the dimension named above; an argument that names none is the same for every part. Nothing has to cross between parts.
All inputs are finite; a program needn't handle non-finite values.
Results may differ from the reference program's by a relative error of at most 0.0044.
Values may be sent and summed in bfloat16 or wider, within the bound.
A program may use at most 64 MiB of HBM per device.

```python
import jax
import jax.numpy as jnp
from jax import lax

CIN = 128
CMID = 256
WIDTH = 512
HEIGHT = 256


def strengthened(values, rng, source, target, blocks, factor):
    def block_of(axis_at):
        return (jnp.arange(values.shape[axis_at]) // (values.shape[axis_at] // blocks)).reshape((-1,) + (1,) * (values.ndim - 1 - axis_at))

    near = jax.random.permutation(rng, blocks)[block_of(target)]
    far = (block_of(target) + blocks // 2) % blocks
    return jnp.where((block_of(source) == near) | (block_of(source) == far), factor * values, values)


def level_of(own_key, shape, cuts, smallest, top_value):
    level, own = 1.0, jax.random.fold_in(own_key, 6)
    for axis_at, blocks in cuts:
        steps = jnp.exp(jax.random.uniform(jax.random.fold_in(own, axis_at), (blocks,), jnp.float32, smallest / len(cuts), top_value / len(cuts)))
        level = level * jnp.repeat(steps, shape[axis_at] // blocks).reshape([-1 if axis == axis_at else 1 for axis in range(len(shape))])
    return level


def scatter_about(own_key, extent, spread, bound, pieces=(), kind=jnp.bfloat16):
    array = spread * jax.random.normal(own_key, extent, jnp.float32)
    if pieces:
        array = array * level_of(own_key, extent, pieces, -0.22, 0.18)
    return jnp.clip(array, -bound, bound).astype(kind)


def gaussian_with(own_key, extent, spread, bound, cuts, heavy, kind=jnp.bfloat16):
    drawn = spread * jax.random.normal(own_key, extent, jnp.float32)
    if cuts:
        drawn = drawn * level_of(own_key, extent, cuts, -0.22, 0.18)
    return jnp.clip(strengthened(drawn, jax.random.fold_in(own_key, 3), *heavy), -bound, bound).astype(kind)


def setup_inputs(seed: int = 0, part: int = 0) -> dict:
    seeds = jax.random.split(jax.random.key(seed), 7)
    part_keys = jax.random.split(jax.random.fold_in(seeds[6], part), 7)
    images = scatter_about(part_keys[0], (HEIGHT, WIDTH, CIN), 1.0, 6.0, ((0, 16),))
    weight_one = scatter_about(seeds[1], (3, 3, CIN, CMID), (9 * CIN) ** -0.5, 0.1875)
    bias_one = scatter_about(seeds[2], (CMID,), 0.5, 3.0, (), jnp.float32)
    weight_two = scatter_about(seeds[3], (3, 3, CMID, CMID), (9 * CMID) ** -0.5, 0.125)
    bias_two = scatter_about(seeds[4], (CMID,), 0.5, 3.0, (), jnp.float32)
    cotangent = gaussian_with(part_keys[5], (HEIGHT // 2, WIDTH // 2, CMID), 0.003, 0.0234375, ((0, 16),), (0, 2, 16, 2.0))
    return {"images": images, "weight_one": weight_one, "bias_one": bias_one, "weight_two": weight_two, "bias_two": bias_two, "cotangent": cotangent}


def convolve(padded, kernel, stride):
    result = lax.conv_general_dilated(padded[None], kernel, (stride, stride), "VALID", dimension_numbers=("NHWC", "HWIO", "NHWC"), preferred_element_type=jnp.float32)
    return result[0]


def tap_grads(source, grad, stride):
    rows_out, cols_out = grad.shape[0], grad.shape[1]
    flat_grad = grad.reshape(-1, grad.shape[2])
    outer = []
    for vertical in range(3):
        inner = []
        for across in range(3):
            patch = source[vertical:vertical + stride * (rows_out - 1) + 1:stride, across:across + stride * (cols_out - 1) + 1:stride]
            flat_patch = patch.reshape(-1, source.shape[2])
            inner.append(jnp.dot(flat_patch.T, flat_grad, preferred_element_type=jnp.float32))
        outer.append(jnp.stack(inner))
    return jnp.stack(outer)


def reference(images, weight_one, bias_one, weight_two, bias_two, cotangent):
    padded_in = jnp.pad(images, ((1, 1), (1, 1), (0, 0)))
    pre_act = convolve(padded_in, weight_one, 2) + bias_one
    hidden = jnp.maximum(pre_act, 0.0).astype(jnp.bfloat16)
    padded_hidden = jnp.pad(hidden, ((1, 1), (1, 1), (0, 0)))
    coarse_out = (convolve(padded_hidden, weight_two, 1) + bias_two).astype(jnp.bfloat16)
    flipped = jnp.transpose(weight_two[::-1, ::-1], (0, 1, 3, 2))
    padded_grad = jnp.pad(cotangent, ((1, 1), (1, 1), (0, 0)))
    grad_hidden = convolve(padded_grad, flipped, 1).astype(jnp.bfloat16)
    grad_pre = jnp.where(pre_act > 0.0, grad_hidden, jnp.zeros_like(grad_hidden))
    grad_w_two = tap_grads(padded_hidden, cotangent, 1)
    grad_b_two = jnp.sum(cotangent.astype(jnp.float32), axis=(0, 1))
    grad_w_one = tap_grads(padded_in, grad_pre, 2)
    grad_b_one = jnp.sum(grad_pre.astype(jnp.float32), axis=(0, 1))
    return (coarse_out, grad_w_one, grad_b_one, grad_w_two, grad_b_two)
```

```python
import functools

import jax
import jax.numpy as jnp
from jax import lax
from jax.experimental import pallas as pl
from jax.experimental.pallas import tpu as pltpu
from jax.sharding import PartitionSpec as P

BF = jnp.bfloat16
F32 = jnp.float32
MESH = pl.DeviceIdType.MESH


def plan(total, order):
    levels, size, offset = [], total, 0
    for distance in order:
        halves = (size // 2) % 16 == 0
        if halves:
            size //= 2
        levels.append((distance, size, halves, offset))
        offset += size
    return levels, offset


def order_of(count):
    near = []
    distance = 1
    while distance < count:
        near.append(distance)
        distance *= 2
    return near, near[:1] + near[2:] + near[1:2]


def remote(src, dst, send, recv, to):
    return pltpu.make_async_remote_copy(
        src_ref=src, dst_ref=dst, send_sem=send, recv_sem=recv, device_id={"row": to}, device_id_type=MESH
    )


class Sum:
    def __init__(self, me, levels, acc, sent, got, full, rs_sems, ag_sems):
        self.me, self.levels = me, levels
        self.acc, self.sent, self.got, self.full = acc, sent, got, full
        self.rs_sems, self.ag_sems = rs_sems, ag_sems
        self.base, self.at = 0, 0
        self.copies, self.keep = [], None
        self.gathers = [i for i, level in enumerate(levels) if level[2]][::-1]

    def rows(self, base, size):
        return pl.ds(base if isinstance(base, int) else pl.multiple_of(base, 16), size)

    def bit(self, level):
        return lax.rem(lax.div(self.me, level[0]), 2)

    def partner(self, level):
        return self.me + level[0] * (1 - 2 * self.bit(level))

    def start(self):
        i = self.at
        level = self.levels[i]
        _, size, halves, offset = level
        bit = self.bit(level)
        own = self.rows(offset, size)
        out = self.base + (1 - bit) * size if halves else self.base
        self.keep = self.base + bit * size if halves else self.base
        self.sent[own] = self.acc[self.rows(out, size)].astype(BF)
        copy = remote(self.sent.at[own], self.got.at[own], self.rs_sems.at[0, i], self.rs_sems.at[1, i], self.partner(level))
        copy.start()
        self.copies.append(copy)

    def finish(self):
        i = self.at
        _, size, halves, offset = self.levels[i]
        self.copies[i].wait()
        own = self.rows(offset, size)
        kept = self.rows(self.keep, size)
        mine = self.acc[kept] if halves else self.sent[own].astype(F32)
        total = mine + self.got[own].astype(F32)
        self.base = self.keep
        self.at += 1
        if self.at == len(self.levels):
            self.full[kept] = total.astype(BF)
            self.gather()
        else:
            self.acc[kept] = total
            self.start()

    def gather(self):
        k = self.at - len(self.levels)
        level = self.levels[self.gathers[k]]
        block = self.full.at[self.rows(self.base, level[1])]
        copy = remote(block, block, self.ag_sems.at[0, k], self.ag_sems.at[1, k], self.partner(level))
        copy.start()
        self.copies.append(copy)

    def gathered(self):
        k = self.at - len(self.levels)
        level = self.levels[self.gathers[k]]
        self.copies[self.at].wait()
        self.base = self.base - self.bit(level) * level[1]
        self.at += 1
        if k + 1 < len(self.gathers):
            self.gather()

    def done(self):
        return self.at == len(self.levels) + len(self.gathers)

    def step(self):
        if self.at < len(self.levels):
            self.finish()
        elif not self.done():
            self.gathered()


def shifted(x):
    wide = x.astype(F32)
    count = x.shape[0]
    row = lax.broadcasted_iota(jnp.int32, x.shape, 0)
    down = jnp.where(row == 0, 0.0, pltpu.roll(wide, 1, 0))
    up = jnp.where(row == count - 1, 0.0, pltpu.roll(wide, count - 1, 0))
    return down.astype(BF), up.astype(BF)


def dot(a, b):
    return jnp.dot(a, b, preferred_element_type=F32)


def kernel(
    count, levels_two, levels_one,
    img_h, w1_h, b1, w2_h, b2, cot_h,
    out, gw1, gw2,
    img, cot, w1, w2, w2t, wide, eo_even, eo_odd, os_even, os_odd,
    himg, hcot, hhid, c3, h3, pre, ht, gt,
    acc2, sent2, got2, full2, acc1, sent1, got1, full1,
    local_sems, halo_sems, rs2, ag2, rs1, ag1,
):
    me = lax.axis_index("row")
    rows, cols = cot_h.shape[0], cot_h.shape[1]
    has_up, has_down = me > 0, me < count - 1
    partners = [me + lv[0] * (1 - 2 * lax.rem(lax.div(me, lv[0]), 2)) for lv in levels_two]

    loads = [
        pltpu.make_async_copy(img_h, img, local_sems.at[0]),
        pltpu.make_async_copy(cot_h, cot, local_sems.at[1]),
        pltpu.make_async_copy(w1_h.at[0, pl.ds(1, 2)], w1.at[pl.ds(0, 2)], local_sems.at[2]),
        pltpu.make_async_copy(w1_h.at[1, pl.ds(1, 2)], w1.at[pl.ds(2, 2)], local_sems.at[3]),
        pltpu.make_async_copy(w1_h.at[2, pl.ds(1, 2)], w1.at[pl.ds(4, 2)], local_sems.at[4]),
        pltpu.make_async_copy(w1_h.at[pl.ds(0, 3), 0], w1.at[pl.ds(6, 3)], local_sems.at[5]),
        pltpu.make_async_copy(w2_h, w2, local_sems.at[6]),
    ]
    for load in loads:
        load.start()

    barrier = pltpu.get_barrier_semaphore()
    for partner in partners:
        pl.semaphore_signal(barrier, inc=1, device_id={"row": partner}, device_id_type=MESH)

    @pl.when(has_up)
    def _():
        pl.semaphore_signal(barrier, inc=1, device_id={"row": me - 1}, device_id_type=MESH)

    @pl.when(has_down)
    def _():
        pl.semaphore_signal(barrier, inc=1, device_id={"row": me + 1}, device_id_type=MESH)

    pl.semaphore_wait(barrier, len(partners) + has_up.astype(jnp.int32) + has_down.astype(jnp.int32))

    down_img = remote(img_h.at[img_h.shape[0] - 1], himg, halo_sems.at[0, 0], halo_sems.at[1, 0], me + 1)
    down_cot = remote(cot_h.at[rows - 1], hcot.at[0], halo_sems.at[0, 1], halo_sems.at[1, 1], me + 1)
    up_cot = remote(cot_h.at[0], hcot.at[1], halo_sems.at[0, 2], halo_sems.at[1, 2], me - 1)
    down_hid = remote(h3.at[rows, :, pl.ds(256, 256)], hhid.at[0], halo_sems.at[0, 3], halo_sems.at[1, 3], me + 1)
    up_hid = remote(h3.at[1, :, pl.ds(256, 256)], hhid.at[1], halo_sems.at[0, 4], halo_sems.at[1, 4], me - 1)

    @pl.when(has_down)
    def _():
        down_img.start()
        down_cot.start()

    @pl.when(has_up)
    def _():
        up_cot.start()

    wide[pl.ds(0, 8)] = jnp.zeros((8, wide.shape[1]), F32)

    def split(x, eo, os, at):
        wide[pl.ds(8, 2 * cols)] = x.astype(F32)
        eo[at, :, pl.ds(0, 128)] = wide[pl.ds(8, cols, stride=2)].astype(BF)
        eo[at, :, pl.ds(128, 128)] = wide[pl.ds(9, cols, stride=2)].astype(BF)
        os[at] = wide[pl.ds(7, cols, stride=2)].astype(BF)

    loads[0].wait()

    def split_pair(o, carry):
        split(img[2 * o], eo_odd, os_odd, o)
        split(img[2 * o + 1], eo_even, os_even, o + 1)
        return carry

    lax.fori_loop(0, rows, split_pair, 0)

    @pl.when(jnp.logical_not(has_up))
    def _():
        himg[...] = jnp.zeros_like(himg)
        hcot[0] = jnp.zeros(hcot.shape[1:], BF)
        hhid[0] = jnp.zeros(hhid.shape[1:], BF)

    @pl.when(jnp.logical_not(has_down))
    def _():
        hcot[1] = jnp.zeros(hcot.shape[1:], BF)
        hhid[1] = jnp.zeros(hhid.shape[1:], BF)

    def put(ref, at, x, flip):
        down, up = shifted(x)
        ref[at, :, pl.ds(0, 256)] = up if flip else down
        ref[at, :, pl.ds(256, 256)] = x
        ref[at, :, pl.ds(512, 256)] = down if flip else up

    loads[1].wait()

    def place_cot(o, carry):
        put(c3, o + 1, cot[o], True)
        return carry

    lax.fori_loop(0, rows, place_cot, 0)
    for load in loads[2:]:
        load.wait()
    for tap in range(9):
        w2t[tap] = w2[tap // 3, tap % 3].T

    @pl.when(has_up)
    def _():
        down_img.wait_recv()
        down_cot.wait_recv()

    @pl.when(has_down)
    def _():
        up_cot.wait_recv()

    split(himg[...], eo_even, os_even, 0)
    put(c3, 0, hcot[0], True)
    put(c3, rows + 1, hcot[1], True)

    block = 2
    size = block * cols

    def flat(ref, at, n=block):
        return ref[pl.ds(at, n)].reshape(n * cols, ref.shape[2])

    def conv_one(i, carry):
        o = i * block
        taps = jnp.concatenate(
            [flat(eo_even, o), flat(eo_odd, o), flat(eo_even, o + 1), flat(os_even, o), flat(os_odd, o), flat(os_even, o + 1)],
            axis=1,
        )
        result = dot(taps, w1[...].reshape(-1, 256)) + b1[...]
        pre[pl.ds(pl.multiple_of(o * cols, size), size)] = result
        hidden = jnp.maximum(result, 0.0).astype(BF)
        for k in range(block):
            one = hidden[k * cols:(k + 1) * cols]
            put(h3, o + k + 1, one, False)
            ht[o + k] = one.T
        return carry

    lax.fori_loop(0, rows // block, conv_one, 0)

    @pl.when(has_down)
    def _():
        down_hid.start()

    @pl.when(has_up)
    def _():
        up_hid.start()

    hidden_t = jnp.concatenate([ht[o] for o in range(rows)], axis=1)
    for a in range(3):
        result = dot(hidden_t, flat(c3, 2 - a, rows))
        for b in range(3):
            acc2[pl.ds((a * 3 + b) * 256, 256)] = result[:, b * 256:(b + 1) * 256]
    two = Sum(me, levels_two, acc2, sent2, got2, full2, rs2, ag2)
    two.start()

    def grad_hidden(i, carry):
        o = i * block
        taps = jnp.concatenate([flat(c3, o + 2), flat(c3, o + 1), flat(c3, o)], axis=1)
        grad = dot(taps, w2t[...].reshape(-1, 256))
        grad = jnp.where(pre[pl.ds(pl.multiple_of(o * cols, size), size)] > 0.0, grad, 0.0).astype(BF)
        for k in range(block):
            gt[o + k] = grad[k * cols:(k + 1) * cols].T
        return carry

    half = rows // block // 2
    lax.fori_loop(0, half, grad_hidden, 0)
    two.step()
    lax.fori_loop(half, rows // block, grad_hidden, 0)

    grad_t = jnp.concatenate([gt[o] for o in range(rows)], axis=1)
    eos = [flat(eo_even, 0, rows), flat(eo_odd, 0, rows), flat(eo_even, 1, rows)]
    for a in range(3):
        acc1[pl.ds((a * 3 + 1) * 128, 256)] = dot(grad_t, eos[a]).T
    ones = jnp.ones((rows * cols, 128), BF)
    last = dot(grad_t, jnp.concatenate([flat(os_even, 0, rows), flat(os_odd, 0, rows), flat(os_even, 1, rows), ones], axis=1)).T
    for a in range(3):
        acc1[pl.ds(a * 384, 128)] = last[a * 128:(a + 1) * 128]
    acc1[pl.ds(1152, 64)] = last[384:448]
    total = jnp.sum(cot[...].reshape(rows * cols, 256).astype(F32), axis=0, keepdims=True)
    acc1[pl.ds(1216, 64)] = jnp.broadcast_to(total, (64, 256))
    one = Sum(me, levels_one, acc1, sent1, got1, full1, rs1, ag1)
    one.start()

    @pl.when(has_up)
    def _():
        down_hid.wait_recv()

    @pl.when(has_down)
    def _():
        up_hid.wait_recv()

    put(h3, 0, hhid[0], False)
    put(h3, rows + 1, hhid[1], False)

    def conv_two(i, carry):
        o = i * block
        taps = jnp.concatenate([flat(h3, o), flat(h3, o + 1), flat(h3, o + 2)], axis=1)
        result = dot(taps, w2[...].reshape(-1, 256)) + b2[...]
        out[pl.ds(o, block)] = result.astype(BF).reshape(block, cols, 256)
        return carry

    lax.fori_loop(0, half, conv_two, 0)
    two.step()
    one.step()
    lax.fori_loop(half, rows // block, conv_two, 0)

    while not (one.done() and two.done()):
        one.step()
        two.step()
    gw1[...] = full1[...]
    gw2[...] = full2[...]

    @pl.when(has_down)
    def _():
        down_img.wait_send()
        down_cot.wait_send()
        down_hid.wait_send()

    @pl.when(has_up)
    def _():
        up_cot.wait_send()
        up_hid.wait_send()


def local(count, images, weight_one, bias_one, weight_two, bias_two, cotangent):
    rows, cols, depth = cotangent.shape
    order_two, order_one = order_of(count)
    levels_two, span_two = plan(9 * depth, order_two)
    levels_one, span_one = plan(9 * images.shape[2] + 128, order_one)
    vmem = pl.BlockSpec(memory_space=pltpu.VMEM)
    hbm = pl.BlockSpec(memory_space=pl.ANY)
    n = len(order_two)
    size_one, size_two = 9 * 128 + 128, 9 * 256
    out, gw1, gw2 = pl.pallas_call(
        functools.partial(kernel, count, levels_two, levels_one),
        out_shape=(
            jax.ShapeDtypeStruct(cotangent.shape, BF),
            jax.ShapeDtypeStruct((size_one, 256), BF),
            jax.ShapeDtypeStruct((size_two, 256), BF),
        ),
        in_specs=[hbm, hbm, vmem, hbm, vmem, hbm],
        out_specs=(vmem, vmem, vmem),
        scratch_shapes=[
            pltpu.VMEM(images.shape, BF),
            pltpu.VMEM(cotangent.shape, BF),
            pltpu.VMEM((9, 128, 256), BF),
            pltpu.VMEM((3, 3, 256, 256), BF),
            pltpu.VMEM((9, 256, 256), BF),
            pltpu.VMEM((2 * cols + 8, 128), F32),
            pltpu.VMEM((rows + 1, cols, 256), BF),
            pltpu.VMEM((rows, cols, 256), BF),
            pltpu.VMEM((rows + 1, cols, 128), BF),
            pltpu.VMEM((rows, cols, 128), BF),
            pltpu.VMEM(images.shape[1:], BF),
            pltpu.VMEM((2, cols, 256), BF),
            pltpu.VMEM((2, cols, 256), BF),
            pltpu.VMEM((rows + 2, cols, 768), BF),
            pltpu.VMEM((rows + 2, cols, 768), BF),
            pltpu.VMEM((rows * cols, 256), F32),
            pltpu.VMEM((rows, 256, cols), BF),
            pltpu.VMEM((rows, 256, cols), BF),
            pltpu.VMEM((size_two, 256), F32),
            pltpu.VMEM((span_two, 256), BF),
            pltpu.VMEM((span_two, 256), BF),
            pltpu.VMEM((size_two, 256), BF),
            pltpu.VMEM((size_one, 256), F32),
            pltpu.VMEM((span_one, 256), BF),
            pltpu.VMEM((span_one, 256), BF),
            pltpu.VMEM((size_one, 256), BF),
            pltpu.SemaphoreType.DMA((7,)),
            pltpu.SemaphoreType.DMA((2, 5)),
            pltpu.SemaphoreType.DMA((2, n)),
            pltpu.SemaphoreType.DMA((2, n)),
            pltpu.SemaphoreType.DMA((2, n)),
            pltpu.SemaphoreType.DMA((2, n)),
        ],
        compiler_params=pltpu.CompilerParams(
            collective_id=0, has_side_effects=True, vmem_limit_bytes=56 * 1024 * 1024
        ),
    )(images, weight_one, bias_one[None], weight_two, bias_two[None], cotangent)
    grads_one = gw1.astype(F32)
    return (
        out,
        grads_one[:1152].reshape(3, 3, 128, 256),
        grads_one[1152],
        gw2.astype(F32).reshape(3, 3, 256, 256),
        grads_one[1216],
    )


def solution(mesh):
    placed = (P(("grp", "row"), None, None), P(), P(), P(), P(), P(("grp", "row"), None, None))
    return jax.shard_map(
        functools.partial(local, mesh.shape["row"]),
        mesh=mesh,
        in_specs=placed,
        out_specs=(
            P(("grp", "row"), None, None),
            P("grp", None, None, None),
            P("grp"),
            P("grp", None, None, None),
            P("grp"),
        ),
        check_vma=False,
    )
```

```python
import functools

import jax
import jax.numpy as jnp
from jax import lax
from jax.experimental import pallas as pl
from jax.experimental.pallas import tpu as pltpu
from jax.sharding import PartitionSpec as P

BF = jnp.bfloat16
F32 = jnp.float32
MESH = pl.DeviceIdType.MESH


def plan(total, order):
    levels, size, offset = [], total, 0
    for distance in order:
        halves = (size // 2) % 16 == 0 and distance != order[-1]
        if halves:
            size //= 2
        levels.append((distance, size, halves, offset))
        offset += size
    return levels, offset


def order_of(count):
    near = []
    distance = 1
    while distance < count:
        near.append(distance)
        distance *= 2
    return near, near[:1] + near[2:] + near[1:2]


def remote(src, dst, send, recv, to):
    return pltpu.make_async_remote_copy(
        src_ref=src, dst_ref=dst, send_sem=send, recv_sem=recv, device_id={"row": to}, device_id_type=MESH
    )


class Sum:
    def __init__(self, me, levels, refs):
        acc, sent, got, full, rs_sems, ag_sems = refs
        self.me, self.levels = me, levels
        self.acc, self.sent, self.got, self.full = acc, sent, got, full
        self.rs_sems, self.ag_sems = rs_sems, ag_sems
        self.base, self.at = 0, 0
        self.copies, self.keep = [], None
        self.gathers = [i for i, level in enumerate(levels) if level[2]][::-1]

    def rows(self, base, size):
        return pl.ds(base if isinstance(base, int) else pl.multiple_of(base, 16), size)

    def bit(self, level):
        return lax.rem(lax.div(self.me, level[0]), 2)

    def partner(self, level):
        return self.me + level[0] * (1 - 2 * self.bit(level))

    def start(self):
        i = self.at
        level = self.levels[i]
        _, size, halves, offset = level
        bit = self.bit(level)
        own = self.rows(offset, size)
        out = self.base + (1 - bit) * size if halves else self.base
        self.keep = self.base + bit * size if halves else self.base
        self.sent[own] = self.acc[self.rows(out, size)].astype(self.sent.dtype)
        copy = remote(self.sent.at[own], self.got.at[own], self.rs_sems.at[0, i], self.rs_sems.at[1, i], self.partner(level))
        copy.start()
        self.copies.append(copy)

    def finish(self):
        i = self.at
        _, size, halves, offset = self.levels[i]
        self.copies[i].wait()
        own = self.rows(offset, size)
        kept = self.rows(self.keep, size)
        mine = self.acc[kept] if halves else self.sent[own].astype(F32)
        total = mine + self.got[own].astype(F32)
        self.base = self.keep
        self.at += 1
        if self.at == len(self.levels):
            self.full[kept] = total.astype(self.full.dtype)
            if self.gathers:
                self.gather()
        else:
            self.acc[kept] = total
            self.start()

    def gather(self):
        k = self.at - len(self.levels)
        level = self.levels[self.gathers[k]]
        block = self.full.at[self.rows(self.base, level[1])]
        copy = remote(block, block, self.ag_sems.at[0, k], self.ag_sems.at[1, k], self.partner(level))
        copy.start()
        self.copies.append(copy)

    def gathered(self):
        k = self.at - len(self.levels)
        level = self.levels[self.gathers[k]]
        self.copies[self.at].wait()
        self.base = self.base - self.bit(level) * level[1]
        self.at += 1
        if k + 1 < len(self.gathers):
            self.gather()

    def done(self):
        return self.at == len(self.levels) + len(self.gathers)

    def step(self):
        if self.at < len(self.levels):
            self.finish()
        elif not self.done():
            self.gathered()


def shifted(x):
    wide = x.astype(F32)
    count = x.shape[0]
    row = lax.broadcasted_iota(jnp.int32, x.shape, 0)
    down = jnp.where(row == 0, 0.0, pltpu.roll(wide, 1, 0))
    up = jnp.where(row == count - 1, 0.0, pltpu.roll(wide, count - 1, 0))
    return down.astype(BF), up.astype(BF)


def dot(a, b):
    return jnp.dot(a, b, preferred_element_type=F32)


def kernel(
    count, plans,
    img_h, w1_h, b1, w2_h, b2, cot_h,
    out_h, gw1_h, gw2_h, biases,
    out, img, cot, w1, w2, w2t, wide, eo_even, eo_odd, os_even, os_odd,
    himg, hcot, hhid, c3, h3, pre, ht, gt,
    local_sems, halo_sems, out_sems, *stream_refs,
):
    me = lax.axis_index("row")
    rows, cols = cot_h.shape[0], cot_h.shape[1]
    has_up, has_down = me > 0, me < count - 1
    partners = [me + lv[0] * (1 - 2 * lax.rem(lax.div(me, lv[0]), 2)) for lv in plans[0]]
    streams = [Sum(me, levels, stream_refs[6 * k:6 * k + 6]) for k, levels in enumerate(plans)]

    loads = [
        pltpu.make_async_copy(img_h, img, local_sems.at[0]),
        pltpu.make_async_copy(cot_h, cot, local_sems.at[1]),
        pltpu.make_async_copy(w1_h.at[0, pl.ds(1, 2)], w1.at[pl.ds(0, 2)], local_sems.at[2]),
        pltpu.make_async_copy(w1_h.at[1, pl.ds(1, 2)], w1.at[pl.ds(2, 2)], local_sems.at[3]),
        pltpu.make_async_copy(w1_h.at[2, pl.ds(1, 2)], w1.at[pl.ds(4, 2)], local_sems.at[4]),
        pltpu.make_async_copy(w1_h.at[pl.ds(0, 3), 0], w1.at[pl.ds(6, 3)], local_sems.at[5]),
        pltpu.make_async_copy(w2_h, w2, local_sems.at[6]),
    ]
    for load in loads:
        load.start()

    barrier = pltpu.get_barrier_semaphore()
    for partner in partners:
        pl.semaphore_signal(barrier, inc=1, device_id={"row": partner}, device_id_type=MESH)

    @pl.when(has_up)
    def _():
        pl.semaphore_signal(barrier, inc=1, device_id={"row": me - 1}, device_id_type=MESH)

    @pl.when(has_down)
    def _():
        pl.semaphore_signal(barrier, inc=1, device_id={"row": me + 1}, device_id_type=MESH)

    pl.semaphore_wait(barrier, len(partners) + has_up.astype(jnp.int32) + has_down.astype(jnp.int32))

    down_img = remote(img_h.at[img_h.shape[0] - 1], himg, halo_sems.at[0, 0], halo_sems.at[1, 0], me + 1)
    down_cot = remote(cot_h.at[rows - 1], hcot.at[0], halo_sems.at[0, 1], halo_sems.at[1, 1], me + 1)
    up_cot = remote(cot_h.at[0], hcot.at[1], halo_sems.at[0, 2], halo_sems.at[1, 2], me - 1)
    down_hid = remote(h3.at[rows, :, pl.ds(256, 256)], hhid.at[0], halo_sems.at[0, 3], halo_sems.at[1, 3], me + 1)
    up_hid = remote(h3.at[1, :, pl.ds(256, 256)], hhid.at[1], halo_sems.at[0, 4], halo_sems.at[1, 4], me - 1)

    @pl.when(has_down)
    def _():
        down_img.start()
        down_cot.start()

    @pl.when(has_up)
    def _():
        up_cot.start()

    wide[pl.ds(0, 8)] = jnp.zeros((8, wide.shape[1]), F32)

    def split(x, eo, os, at):
        wide[pl.ds(8, 2 * cols)] = x.astype(F32)
        eo[at, :, pl.ds(0, 128)] = wide[pl.ds(8, cols, stride=2)].astype(BF)
        eo[at, :, pl.ds(128, 128)] = wide[pl.ds(9, cols, stride=2)].astype(BF)
        os[at] = wide[pl.ds(7, cols, stride=2)].astype(BF)

    loads[0].wait()

    def split_pair(o, carry):
        split(img[2 * o], eo_odd, os_odd, o)
        split(img[2 * o + 1], eo_even, os_even, o + 1)
        return carry

    lax.fori_loop(0, rows, split_pair, 0)

    @pl.when(jnp.logical_not(has_up))
    def _():
        himg[...] = jnp.zeros_like(himg)
        hcot[0] = jnp.zeros(hcot.shape[1:], BF)
        hhid[0] = jnp.zeros(hhid.shape[1:], BF)

    @pl.when(jnp.logical_not(has_down))
    def _():
        hcot[1] = jnp.zeros(hcot.shape[1:], BF)
        hhid[1] = jnp.zeros(hhid.shape[1:], BF)

    def put(ref, at, x, flip):
        down, up = shifted(x)
        ref[at, :, pl.ds(0, 256)] = up if flip else down
        ref[at, :, pl.ds(256, 256)] = x
        ref[at, :, pl.ds(512, 256)] = down if flip else up

    loads[1].wait()

    def place_cot(o, carry):
        put(c3, o + 1, cot[o], True)
        return carry

    lax.fori_loop(0, rows, place_cot, 0)
    for load in loads[2:]:
        load.wait()
    for tap in range(9):
        w2t[tap] = w2[tap // 3, tap % 3].T

    block = 2
    size = block * cols

    def flat(ref, at, n=block):
        return ref[pl.ds(at, n)].reshape(n * cols, ref.shape[2])

    def conv_one(i, carry):
        o = i * block
        taps = jnp.concatenate(
            [flat(eo_even, o), flat(eo_odd, o), flat(eo_even, o + 1), flat(os_even, o), flat(os_odd, o), flat(os_even, o + 1)],
            axis=1,
        )
        result = dot(taps, w1[...].reshape(-1, 256)) + b1[...]
        pre[pl.ds(pl.multiple_of(o * cols, size), size)] = result
        hidden = jnp.maximum(result, 0.0).astype(BF)
        for k in range(block):
            one = hidden[k * cols:(k + 1) * cols]
            put(h3, o + k + 1, one, False)
            ht[o + k] = one.T
        return carry

    def grad_hidden(i, carry):
        o = i * block
        taps = jnp.concatenate([flat(c3, o + 2), flat(c3, o + 1), flat(c3, o)], axis=1)
        grad = dot(taps, w2t[...].reshape(-1, 256))
        grad = jnp.where(pre[pl.ds(pl.multiple_of(o * cols, size), size)] > 0.0, grad, 0.0).astype(BF)
        for k in range(block):
            gt[o + k] = grad[k * cols:(k + 1) * cols].T
        return carry

    def conv_two(i, carry):
        o = i * block
        taps = jnp.concatenate([flat(h3, o), flat(h3, o + 1), flat(h3, o + 2)], axis=1)
        result = dot(taps, w2[...].reshape(-1, 256)) + b2[...]
        out[pl.ds(o, block)] = result.astype(BF).reshape(block, cols, 256)
        return carry

    blocks = rows // block

    def work(first, last, body):
        lax.fori_loop(first, last, body, 0)

    work(1, blocks, conv_one)
    work(1, blocks - 1, grad_hidden)

    @pl.when(has_up)
    def _():
        down_img.wait_recv()

    split(himg[...], eo_even, os_even, 0)
    work(0, 1, conv_one)

    @pl.when(has_down)
    def _():
        down_hid.start()

    @pl.when(has_up)
    def _():
        up_hid.start()

    hidden_t = jnp.concatenate([ht[o] for o in range(rows)], axis=1)

    def taps_two(a):
        result = dot(hidden_t, flat(c3, 2 - a, rows))
        for b in range(3):
            streams[a].acc[pl.ds(b * 256, 256)] = result[:, b * 256:(b + 1) * 256]
        streams[a].start()

    taps_two(1)

    @pl.when(has_up)
    def _():
        down_cot.wait_recv()

    put(c3, 0, hcot[0], True)
    taps_two(2)

    @pl.when(has_down)
    def _():
        up_cot.wait_recv()

    put(c3, rows + 1, hcot[1], True)
    streams[1].step()
    taps_two(0)
    work(0, 1, grad_hidden)
    streams[2].step()
    work(blocks - 1, blocks, grad_hidden)
    streams[0].step()

    grad_t = jnp.concatenate([gt[o] for o in range(rows)], axis=1)
    eos = [flat(eo_even, 0, rows), flat(eo_odd, 0, rows), flat(eo_even, 1, rows)]
    acc1 = streams[3].acc
    for a in range(3):
        acc1[pl.ds((a * 3 + 1) * 128, 256)] = dot(grad_t, eos[a]).T
    ones = jnp.ones((rows * cols, 128), BF)
    last = dot(grad_t, jnp.concatenate([flat(os_even, 0, rows), flat(os_odd, 0, rows), flat(os_even, 1, rows), ones], axis=1)).T
    for a in range(3):
        acc1[pl.ds(a * 384, 128)] = last[a * 128:(a + 1) * 128]
    streams[3].start()
    streams[1].step()
    streams[4].acc[pl.ds(0, 8)] = last[384:392]
    total = jnp.sum(cot[...].reshape(rows * cols, 256).astype(F32), axis=0, keepdims=True)
    streams[4].acc[pl.ds(8, 8)] = jnp.broadcast_to(total, (8, 256))
    streams[4].start()

    @pl.when(has_up)
    def _():
        down_hid.wait_recv()

    @pl.when(has_down)
    def _():
        up_hid.wait_recv()

    put(h3, 0, hhid[0], False)
    put(h3, rows + 1, hhid[1], False)
    work(0, 1, conv_two)
    streams[2].step()
    streams[3].step()
    work(1, 2, conv_two)
    streams[1].step()
    streams[0].step()
    streams[4].step()
    work(2, 3, conv_two)
    streams[2].step()
    work(3, blocks, conv_two)

    results = [gw2_h.at[pl.ds(a * 768, 768)] for a in range(3)] + [gw1_h]
    stores = [pltpu.make_async_copy(out, out_h, out_sems.at[4])]
    stores[0].start()
    stored = set()
    while len(stored) < 5:
        for k in (1, 2, 0, 3, 4):
            streams[k].step()
            if streams[k].done() and k not in stored:
                stored.add(k)
                if k < 4:
                    stores.append(pltpu.make_async_copy(streams[k].full, results[k], out_sems.at[k]))
                    stores[-1].start()
    biases[...] = streams[4].full[...]
    for store in stores:
        store.wait()

    @pl.when(has_down)
    def _():
        down_img.wait_send()
        down_cot.wait_send()
        down_hid.wait_send()

    @pl.when(has_up)
    def _():
        up_cot.wait_send()
        up_hid.wait_send()


def local(count, images, weight_one, bias_one, weight_two, bias_two, cotangent):
    rows, cols, depth = cotangent.shape
    y_first, z_first = order_of(count)
    totals = (768, 768, 768, 1152, 16)
    planned = [plan(size, z_first if k == 1 else y_first) for k, size in enumerate(totals)]
    n = len(y_first)
    stream_shapes = []
    for k, (size, (_, span)) in enumerate(zip(totals, planned)):
        kind = F32 if k == 4 else BF
        stream_shapes += [
            pltpu.VMEM((size, 256), F32),
            pltpu.VMEM((span, 256), kind),
            pltpu.VMEM((span, 256), kind),
            pltpu.VMEM((size, 256), kind),
            pltpu.SemaphoreType.DMA((2, n)),
            pltpu.SemaphoreType.DMA((2, n)),
        ]
    vmem = pl.BlockSpec(memory_space=pltpu.VMEM)
    hbm = pl.BlockSpec(memory_space=pl.ANY)
    size_one, size_two = 9 * 128, 9 * 256
    out, gw1, gw2, biases = pl.pallas_call(
        functools.partial(kernel, count, [levels for levels, _ in planned]),
        out_shape=(
            jax.ShapeDtypeStruct(cotangent.shape, BF),
            jax.ShapeDtypeStruct((size_one, 256), BF),
            jax.ShapeDtypeStruct((size_two, 256), BF),
            jax.ShapeDtypeStruct((16, 256), F32),
        ),
        in_specs=[hbm, hbm, vmem, hbm, vmem, hbm],
        out_specs=(hbm, hbm, hbm, vmem),
        scratch_shapes=[
            pltpu.VMEM(cotangent.shape, BF),
            pltpu.VMEM(images.shape, BF),
            pltpu.VMEM(cotangent.shape, BF),
            pltpu.VMEM((9, 128, 256), BF),
            pltpu.VMEM((3, 3, 256, 256), BF),
            pltpu.VMEM((9, 256, 256), BF),
            pltpu.VMEM((2 * cols + 8, 128), F32),
            pltpu.VMEM((rows + 1, cols, 256), BF),
            pltpu.VMEM((rows, cols, 256), BF),
            pltpu.VMEM((rows + 1, cols, 128), BF),
            pltpu.VMEM((rows, cols, 128), BF),
            pltpu.VMEM(images.shape[1:], BF),
            pltpu.VMEM((2, cols, 256), BF),
            pltpu.VMEM((2, cols, 256), BF),
            pltpu.VMEM((rows + 2, cols, 768), BF),
            pltpu.VMEM((rows + 2, cols, 768), BF),
            pltpu.VMEM((rows * cols, 256), F32),
            pltpu.VMEM((rows, 256, cols), BF),
            pltpu.VMEM((rows, 256, cols), BF),
            pltpu.SemaphoreType.DMA((7,)),
            pltpu.SemaphoreType.DMA((2, 5)),
            pltpu.SemaphoreType.DMA((5,)),
            *stream_shapes,
        ],
        compiler_params=pltpu.CompilerParams(
            collective_id=0, has_side_effects=True, vmem_limit_bytes=56 * 1024 * 1024
        ),
    )(images, weight_one, bias_one[None], weight_two, bias_two[None], cotangent)
    return (
        out,
        gw1.astype(F32).reshape(3, 3, 128, 256),
        biases[0],
        gw2.astype(F32).reshape(3, 3, 256, 256),
        biases[8],
    )


def solution(mesh):
    placed = (P(("grp", "row"), None, None), P(), P(), P(), P(), P(("grp", "row"), None, None))
    return jax.shard_map(
        functools.partial(local, mesh.shape["row"]),
        mesh=mesh,
        in_specs=placed,
        out_specs=(
            P(("grp", "row"), None, None),
            P("grp", None, None, None),
            P("grp"),
            P("grp", None, None, None),
            P("grp"),
        ),
        check_vma=False,
    )
```

```python
import functools

import jax
import jax.numpy as jnp
from jax import lax
from jax.experimental import pallas as pl
from jax.experimental.pallas import tpu as pltpu
from jax.sharding import PartitionSpec as P

BF = jnp.bfloat16
F32 = jnp.float32
MESH = pl.DeviceIdType.MESH


def plan(total, order):
    levels, size, offset = [], total, 0
    for distance in order:
        halves = (size // 2) % 16 == 0 and distance != order[-1]
        if halves:
            size //= 2
        levels.append((distance, size, halves, offset))
        offset += size
    return levels, offset


def order_of(count):
    near = []
    distance = 1
    while distance < count:
        near.append(distance)
        distance *= 2
    return near


def remote(src, dst, send, recv, to):
    return pltpu.make_async_remote_copy(
        src_ref=src, dst_ref=dst, send_sem=send, recv_sem=recv, device_id={"row": to}, device_id_type=MESH
    )


class Sum:
    def __init__(self, me, levels, refs):
        acc, sent, got, full, rs_sems, ag_sems = refs
        self.me, self.levels = me, levels
        self.acc, self.sent, self.got, self.full = acc, sent, got, full
        self.rs_sems, self.ag_sems = rs_sems, ag_sems
        self.base, self.at = 0, 0
        self.copies, self.keep = [], None
        self.gathers = [i for i, level in enumerate(levels) if level[2]][::-1]

    def rows(self, base, size):
        return pl.ds(base if isinstance(base, int) else pl.multiple_of(base, 16), size)

    def bit(self, level):
        return lax.rem(lax.div(self.me, level[0]), 2)

    def partner(self, level):
        return self.me + level[0] * (1 - 2 * self.bit(level))

    def start(self):
        i = self.at
        level = self.levels[i]
        _, size, halves, offset = level
        bit = self.bit(level)
        own = self.rows(offset, size)
        out = self.base + (1 - bit) * size if halves else self.base
        self.keep = self.base + bit * size if halves else self.base
        self.sent[own] = self.acc[self.rows(out, size)].astype(self.sent.dtype)
        copy = remote(self.sent.at[own], self.got.at[own], self.rs_sems.at[0, i], self.rs_sems.at[1, i], self.partner(level))
        copy.start()
        self.copies.append(copy)

    def finish(self):
        i = self.at
        _, size, halves, offset = self.levels[i]
        self.copies[i].wait()
        own = self.rows(offset, size)
        kept = self.rows(self.keep, size)
        mine = self.acc[kept] if halves else self.sent[own].astype(F32)
        total = mine + self.got[own].astype(F32)
        self.base = self.keep
        self.at += 1
        if self.at == len(self.levels):
            self.full[kept] = total.astype(self.full.dtype)
            if self.gathers:
                self.gather()
        else:
            self.acc[kept] = total
            self.start()

    def gather(self):
        k = self.at - len(self.levels)
        level = self.levels[self.gathers[k]]
        block = self.full.at[self.rows(self.base, level[1])]
        copy = remote(block, block, self.ag_sems.at[0, k], self.ag_sems.at[1, k], self.partner(level))
        copy.start()
        self.copies.append(copy)

    def gathered(self):
        k = self.at - len(self.levels)
        level = self.levels[self.gathers[k]]
        self.copies[self.at].wait()
        self.base = self.base - self.bit(level) * level[1]
        self.at += 1
        if k + 1 < len(self.gathers):
            self.gather()

    def done(self):
        return self.at == len(self.levels) + len(self.gathers)

    def step(self):
        if self.at < len(self.levels):
            self.finish()
        elif not self.done():
            self.gathered()


def shifted(x):
    wide = x.astype(F32)
    count = x.shape[0]
    row = lax.broadcasted_iota(jnp.int32, x.shape, 0)
    down = jnp.where(row == 0, 0.0, pltpu.roll(wide, 1, 0))
    up = jnp.where(row == count - 1, 0.0, pltpu.roll(wide, count - 1, 0))
    return down.astype(BF), up.astype(BF)


def dot(a, b):
    return jnp.dot(a, b, preferred_element_type=F32)


def kernel(
    count, plans,
    img_h, w1_h, b1, w2_h, b2, cot_h,
    out_h, gw1_h, gw2_h, biases,
    out, img, cot, w1, w2, w2t, wide, eo_even, eo_odd, os_even, os_odd,
    himg, hcot, hhid, c3, h3, pre, ht, gt,
    local_sems, halo_sems, out_sems, *stream_refs,
):
    me = lax.axis_index("row")
    rows, cols = cot_h.shape[0], cot_h.shape[1]
    has_up, has_down = me > 0, me < count - 1
    partners = [me + lv[0] * (1 - 2 * lax.rem(lax.div(me, lv[0]), 2)) for lv in plans[0]]
    streams = [Sum(me, levels, stream_refs[6 * k:6 * k + 6]) for k, levels in enumerate(plans)]

    loads = [
        pltpu.make_async_copy(img_h, img, local_sems.at[0]),
        pltpu.make_async_copy(cot_h, cot, local_sems.at[1]),
        pltpu.make_async_copy(w1_h.at[0, pl.ds(1, 2)], w1.at[pl.ds(0, 2)], local_sems.at[2]),
        pltpu.make_async_copy(w1_h.at[1, pl.ds(1, 2)], w1.at[pl.ds(2, 2)], local_sems.at[3]),
        pltpu.make_async_copy(w1_h.at[2, pl.ds(1, 2)], w1.at[pl.ds(4, 2)], local_sems.at[4]),
        pltpu.make_async_copy(w1_h.at[pl.ds(0, 3), 0], w1.at[pl.ds(6, 3)], local_sems.at[5]),
        pltpu.make_async_copy(w2_h, w2, local_sems.at[6]),
    ]
    for load in loads:
        load.start()

    barrier = pltpu.get_barrier_semaphore()
    for partner in partners:
        pl.semaphore_signal(barrier, inc=1, device_id={"row": partner}, device_id_type=MESH)

    @pl.when(has_up)
    def _():
        pl.semaphore_signal(barrier, inc=1, device_id={"row": me - 1}, device_id_type=MESH)

    @pl.when(has_down)
    def _():
        pl.semaphore_signal(barrier, inc=1, device_id={"row": me + 1}, device_id_type=MESH)

    pl.semaphore_wait(barrier, len(partners) + has_up.astype(jnp.int32) + has_down.astype(jnp.int32))

    down_img = remote(img_h.at[img_h.shape[0] - 1], himg, halo_sems.at[0, 0], halo_sems.at[1, 0], me + 1)
    down_cot = remote(cot_h.at[rows - 1], hcot.at[0], halo_sems.at[0, 1], halo_sems.at[1, 1], me + 1)
    up_cot = remote(cot_h.at[0], hcot.at[1], halo_sems.at[0, 2], halo_sems.at[1, 2], me - 1)
    down_hid = remote(h3.at[rows, :, pl.ds(256, 256)], hhid.at[0], halo_sems.at[0, 3], halo_sems.at[1, 3], me + 1)
    up_hid = remote(h3.at[1, :, pl.ds(256, 256)], hhid.at[1], halo_sems.at[0, 4], halo_sems.at[1, 4], me - 1)

    @pl.when(has_down)
    def _():
        down_img.start()
        down_cot.start()

    @pl.when(has_up)
    def _():
        up_cot.start()

    wide[pl.ds(0, 8)] = jnp.zeros((8, wide.shape[1]), F32)

    def split(x, eo, os, at):
        wide[pl.ds(8, 2 * cols)] = x.astype(F32)
        eo[at, :, pl.ds(0, 128)] = wide[pl.ds(8, cols, stride=2)].astype(BF)
        eo[at, :, pl.ds(128, 128)] = wide[pl.ds(9, cols, stride=2)].astype(BF)
        os[at] = wide[pl.ds(7, cols, stride=2)].astype(BF)

    loads[0].wait()

    def split_pair(o, carry):
        split(img[2 * o], eo_odd, os_odd, o)
        split(img[2 * o + 1], eo_even, os_even, o + 1)
        return carry

    lax.fori_loop(0, rows, split_pair, 0)

    @pl.when(jnp.logical_not(has_up))
    def _():
        himg[...] = jnp.zeros_like(himg)
        hcot[0] = jnp.zeros(hcot.shape[1:], BF)
        hhid[0] = jnp.zeros(hhid.shape[1:], BF)

    @pl.when(jnp.logical_not(has_down))
    def _():
        hcot[1] = jnp.zeros(hcot.shape[1:], BF)
        hhid[1] = jnp.zeros(hhid.shape[1:], BF)

    def put(ref, at, x, flip):
        down, up = shifted(x)
        ref[at, :, pl.ds(0, 256)] = up if flip else down
        ref[at, :, pl.ds(256, 256)] = x
        ref[at, :, pl.ds(512, 256)] = down if flip else up

    loads[1].wait()

    def place_cot(o, carry):
        put(c3, o + 1, cot[o], True)
        return carry

    lax.fori_loop(0, rows, place_cot, 0)
    for load in loads[2:]:
        load.wait()
    for tap in range(9):
        w2t[tap] = w2[tap // 3, tap % 3].T

    block = 2
    size = block * cols

    def flat(ref, at, n=block):
        return ref[pl.ds(at, n)].reshape(n * cols, ref.shape[2])

    def conv_one(i, carry):
        o = i * block
        taps = jnp.concatenate(
            [flat(eo_even, o), flat(eo_odd, o), flat(eo_even, o + 1), flat(os_even, o), flat(os_odd, o), flat(os_even, o + 1)],
            axis=1,
        )
        result = dot(taps, w1[...].reshape(-1, 256)) + b1[...]
        pre[pl.ds(pl.multiple_of(o * cols, size), size)] = result
        hidden = jnp.maximum(result, 0.0).astype(BF)
        for k in range(block):
            one = hidden[k * cols:(k + 1) * cols]
            put(h3, o + k + 1, one, False)
            ht[o + k] = one.T
        return carry

    def grad_hidden(i, carry):
        o = i * block
        taps = jnp.concatenate([flat(c3, o + 2), flat(c3, o + 1), flat(c3, o)], axis=1)
        grad = dot(taps, w2t[...].reshape(-1, 256))
        grad = jnp.where(pre[pl.ds(pl.multiple_of(o * cols, size), size)] > 0.0, grad, 0.0).astype(BF)
        for k in range(block):
            gt[o + k] = grad[k * cols:(k + 1) * cols].T
        return carry

    def conv_two(i, carry):
        o = i * block
        taps = jnp.concatenate([flat(h3, o), flat(h3, o + 1), flat(h3, o + 2)], axis=1)
        result = dot(taps, w2[...].reshape(-1, 256)) + b2[...]
        out[pl.ds(o, block)] = result.astype(BF).reshape(block, cols, 256)
        return carry

    blocks = rows // block

    def work(first, last, body):
        lax.fori_loop(first, last, body, 0)

    work(1, blocks, conv_one)
    work(1, blocks - 1, grad_hidden)

    @pl.when(has_up)
    def _():
        down_img.wait_recv()

    split(himg[...], eo_even, os_even, 0)
    work(0, 1, conv_one)

    @pl.when(has_down)
    def _():
        down_hid.start()

    @pl.when(has_up)
    def _():
        up_hid.start()

    hidden_t = jnp.concatenate([ht[o] for o in range(rows)], axis=1)

    def taps_two(a):
        result = dot(hidden_t, flat(c3, 2 - a, rows))
        for b in range(3):
            streams[a].acc[pl.ds(b * 256, 256)] = result[:, b * 256:(b + 1) * 256]
        streams[a].start()

    taps_two(1)

    @pl.when(has_up)
    def _():
        down_cot.wait_recv()

    put(c3, 0, hcot[0], True)
    taps_two(2)

    @pl.when(has_down)
    def _():
        up_cot.wait_recv()

    put(c3, rows + 1, hcot[1], True)
    streams[1].step()
    taps_two(0)
    work(0, 1, grad_hidden)
    streams[2].step()
    work(blocks - 1, blocks, grad_hidden)
    streams[0].step()

    grad_t = jnp.concatenate([gt[o] for o in range(rows)], axis=1)
    eos = [flat(eo_even, 0, rows), flat(eo_odd, 0, rows), flat(eo_even, 1, rows)]
    acc1 = streams[3].acc
    for a in range(3):
        acc1[pl.ds((a * 3 + 1) * 128, 256)] = dot(grad_t, eos[a]).T
    ones = jnp.ones((rows * cols, 128), BF)
    last = dot(grad_t, jnp.concatenate([flat(os_even, 0, rows), flat(os_odd, 0, rows), flat(os_even, 1, rows), ones], axis=1)).T
    for a in range(3):
        acc1[pl.ds(a * 384, 128)] = last[a * 128:(a + 1) * 128]
    streams[3].start()
    streams[1].step()
    streams[4].acc[pl.ds(0, 8)] = last[384:392]
    total = jnp.sum(cot[...].reshape(rows * cols, 256).astype(F32), axis=0, keepdims=True)
    streams[4].acc[pl.ds(8, 8)] = jnp.broadcast_to(total, (8, 256))
    streams[4].start()

    @pl.when(has_up)
    def _():
        down_hid.wait_recv()

    @pl.when(has_down)
    def _():
        up_hid.wait_recv()

    put(h3, 0, hhid[0], False)
    put(h3, rows + 1, hhid[1], False)
    work(0, 1, conv_two)
    streams[2].step()
    streams[3].step()
    work(1, 2, conv_two)
    streams[1].step()
    streams[0].step()
    streams[4].step()
    work(2, 3, conv_two)
    streams[2].step()
    work(3, blocks, conv_two)

    results = [gw2_h.at[pl.ds(a * 768, 768)] for a in range(3)] + [gw1_h]
    stores = [pltpu.make_async_copy(out, out_h, out_sems.at[4])]
    stores[0].start()
    stored = set()
    while len(stored) < 5:
        for k in (1, 2, 0, 3, 4):
            streams[k].step()
            if streams[k].done() and k not in stored:
                stored.add(k)
                if k < 4:
                    stores.append(pltpu.make_async_copy(streams[k].full, results[k], out_sems.at[k]))
                    stores[-1].start()
    biases[...] = streams[4].full[...]
    for store in stores:
        store.wait()

    @pl.when(has_down)
    def _():
        down_img.wait_send()
        down_cot.wait_send()
        down_hid.wait_send()

    @pl.when(has_up)
    def _():
        up_cot.wait_send()
        up_hid.wait_send()


def local(count, images, weight_one, bias_one, weight_two, bias_two, cotangent):
    rows, cols, depth = cotangent.shape
    y_first = order_of(count)
    totals = (768, 768, 768, 1152, 16)
    planned = [plan(size, y_first) for k, size in enumerate(totals)]
    n = len(y_first)
    stream_shapes = []
    for k, (size, (_, span)) in enumerate(zip(totals, planned)):
        kind = F32 if k == 4 else BF
        stream_shapes += [
            pltpu.VMEM((size, 256), F32),
            pltpu.VMEM((span, 256), kind),
            pltpu.VMEM((span, 256), kind),
            pltpu.VMEM((size, 256), kind),
            pltpu.SemaphoreType.DMA((2, n)),
            pltpu.SemaphoreType.DMA((2, n)),
        ]
    vmem = pl.BlockSpec(memory_space=pltpu.VMEM)
    hbm = pl.BlockSpec(memory_space=pl.ANY)
    size_one, size_two = 9 * 128, 9 * 256
    out, gw1, gw2, biases = pl.pallas_call(
        functools.partial(kernel, count, [levels for levels, _ in planned]),
        out_shape=(
            jax.ShapeDtypeStruct(cotangent.shape, BF),
            jax.ShapeDtypeStruct((size_one, 256), BF),
            jax.ShapeDtypeStruct((size_two, 256), BF),
            jax.ShapeDtypeStruct((16, 256), F32),
        ),
        in_specs=[hbm, hbm, vmem, hbm, vmem, hbm],
        out_specs=(hbm, hbm, hbm, vmem),
        scratch_shapes=[
            pltpu.VMEM(cotangent.shape, BF),
            pltpu.VMEM(images.shape, BF),
            pltpu.VMEM(cotangent.shape, BF),
            pltpu.VMEM((9, 128, 256), BF),
            pltpu.VMEM((3, 3, 256, 256), BF),
            pltpu.VMEM((9, 256, 256), BF),
            pltpu.VMEM((2 * cols + 8, 128), F32),
            pltpu.VMEM((rows + 1, cols, 256), BF),
            pltpu.VMEM((rows, cols, 256), BF),
            pltpu.VMEM((rows + 1, cols, 128), BF),
            pltpu.VMEM((rows, cols, 128), BF),
            pltpu.VMEM(images.shape[1:], BF),
            pltpu.VMEM((2, cols, 256), BF),
            pltpu.VMEM((2, cols, 256), BF),
            pltpu.VMEM((rows + 2, cols, 768), BF),
            pltpu.VMEM((rows + 2, cols, 768), BF),
            pltpu.VMEM((rows * cols, 256), F32),
            pltpu.VMEM((rows, 256, cols), BF),
            pltpu.VMEM((rows, 256, cols), BF),
            pltpu.SemaphoreType.DMA((7,)),
            pltpu.SemaphoreType.DMA((2, 5)),
            pltpu.SemaphoreType.DMA((5,)),
            *stream_shapes,
        ],
        compiler_params=pltpu.CompilerParams(
            collective_id=0, has_side_effects=True, vmem_limit_bytes=56 * 1024 * 1024
        ),
    )(images, weight_one, bias_one[None], weight_two, bias_two[None], cotangent)
    return (
        out,
        gw1.astype(F32).reshape(3, 3, 128, 256),
        biases[0],
        gw2.astype(F32).reshape(3, 3, 256, 256),
        biases[8],
    )


def solution(mesh):
    placed = (P(("grp", "row"), None, None), P(), P(), P(), P(), P(("grp", "row"), None, None))
    return jax.shard_map(
        functools.partial(local, mesh.shape["row"]),
        mesh=mesh,
        in_specs=placed,
        out_specs=(
            P(("grp", "row"), None, None),
            P("grp", None, None, None),
            P("grp"),
            P("grp", None, None, None),
            P("grp"),
        ),
        check_vma=False,
    )
```
